256 devices in a mesh: row: 32 (over z, x), col: 8 (over y, core).
Axes of the slice: x: 4, y: 4, z: 8, core: 2. Of those that a mesh axis runs over, the one named last changes fastest.
Arguments:
- moving_slab: float32 [32, 512, 1024], P('row', None, 'col'), may hold values from -6 to 6
- fixed_image: float32 [32, 512, 1024], P(None, 'row', 'col'), may hold values from -6 to 6
- start_field: float32 [3, 32, 512, 1024], P(None, None, 'row', 'col'), may hold values from -6 to 6
- tissue_mask: int32 [4, 32, 8], replicated, may hold values 0 or 1
Outputs:
- displacement: float32 [3, 32, 512, 1024], P(None, None, 'row', 'col')
The draws below stay inside these ranges and needn't reach their ends.
All inputs are finite; a program needn't handle non-finite values.
Results may differ from the reference program's by a relative error of at most 0.000084.
Values sent between devices are 32-bit elements; how exact they have to be, the bound alone decides.
No kernel may reach another device: no remote copies, remote signals or barrier semaphores. Data moves between devices by JAX's collectives and lax.ppermute only.
A program may use at most 64 MiB of HBM per device.

```python
import jax
import jax.numpy as jnp

CY = 16
CX = 128
KZ = 4
ITERS = 3
NZ = 32
NY = 512
NX = 1024
BRICK_ROWS = 32
BRICK_COLS = 8


def plant(values, own_key, low, largest):
    index_at = [jax.random.randint(jax.random.fold_in(own_key, axis), (), 0, length) for axis, length in enumerate(values.shape)]
    longest = values.shape.index(max(values.shape))
    beside = index_at[:longest] + [(index_at[longest] + 1) % values.shape[longest]] + index_at[longest + 1:]
    return values.at[tuple(index_at)].set(low).at[tuple(beside)].set(largest)


def block_levels(rng, dims, shards, low, top_value):
    def one(dim, shards_of):
        steps = jax.random.uniform(jax.random.fold_in(jax.random.fold_in(rng, 6), dim), (shards_of,), jnp.float32, low / len(shards), top_value / len(shards))
        return jnp.repeat(jnp.exp(steps), dims[dim] // shards_of).reshape((-1,) + (1,) * (len(dims) - dim - 1))

    factor_of = one(*shards[0])
    for cut in shards[1:]:
        factor_of = factor_of * one(*cut)
    return factor_of


def noise(stream_key, shape, spread, reach, cuts=(), held_as=jnp.bfloat16):
    level = block_levels(stream_key, shape, cuts, -0.22, 0.18) if cuts else 1.0
    entries = jax.random.normal(stream_key, shape, jnp.float32) * spread * level
    return jnp.minimum(jnp.maximum(entries, -reach), reach).astype(held_as)


def setup_inputs(seed: int = 0) -> dict:
    streams_of = jax.random.split(jax.random.key(seed), 5)
    return {
        "moving_slab": noise(streams_of[0], (NZ, NY, NX), 1.0, 6.0, ((0, 32), (2, 8)), jnp.float32),
        "fixed_image": noise(streams_of[1], (NZ, NY, NX), 1.0, 6.0, ((1, 32), (2, 8)), jnp.float32),
        "start_field": noise(streams_of[2], (3, NZ, NY, NX), 1.0, 6.0, ((2, 32), (3, 8)), jnp.float32),
        "tissue_mask": plant((jax.random.randint(streams_of[3], (KZ, BRICK_ROWS, BRICK_COLS), 0, 4) < 3).astype(jnp.int32), jax.random.fold_in(streams_of[3], 1), 0, 1),
    }


pull_rate = 1.0
smooth_rate = 0.16


def gradient(extended):
    padded = jnp.pad(extended[:, 1:-1, 1:-1], ((1, 1), (0, 0), (0, 0)))
    grad_z = 0.5 * (padded[2:] - padded[:-2])
    grad_y = 0.5 * (extended[:, 2:, 1:-1] - extended[:, :-2, 1:-1])
    grad_x = 0.5 * (extended[:, 1:-1, 2:] - extended[:, 1:-1, :-2])
    return jnp.stack([grad_z, grad_y, grad_x])


def attract(displace, slopes, fixed, moving, tissue):
    residual = fixed - moving - (slopes[0] * displace[0] + slopes[1] * displace[1] + slopes[2] * displace[2])
    denominator = slopes[0] * slopes[0] + slopes[1] * slopes[1] + slopes[2] * slopes[2] + residual * residual + 0.5
    return tissue * (displace + pull_rate * residual * slopes / denominator)


def window(array, shift_z, shift_y, shift_x):
    extent_z, extent_y, extent_x = array.shape[-3:]
    return array[..., 1 + shift_z:extent_z - 1 + shift_z, 1 + shift_y:extent_y - 1 + shift_y, 1 + shift_x:extent_x - 1 + shift_x]


def smooth(extended, tissue_rim):
    field_pad = jnp.pad(extended, ((0, 0), (1, 1), (0, 0), (0, 0)))
    tissue_pad = jnp.pad(tissue_rim, ((1, 1), (0, 0), (0, 0)))
    centre = window(field_pad, 0, 0, 0)
    centre_tissue = window(tissue_pad, 0, 0, 0)
    flow = jnp.zeros_like(centre)
    for offset in ((1, 0, 0), (-1, 0, 0), (0, 1, 0), (0, -1, 0), (0, 0, 1), (0, 0, -1)):
        flow = flow + window(tissue_pad, *offset) * (window(field_pad, *offset) - centre)
    return centre + smooth_rate * centre_tissue * flow


def reference(moving_slab, fixed_image, start_field, tissue_mask):
    table = tissue_mask.astype(jnp.float32)
    tissue = jnp.repeat(jnp.repeat(jnp.repeat(table, NZ // KZ, axis=0), CY, axis=1), CX, axis=2)
    slopes = gradient(jnp.pad(moving_slab, ((0, 0), (1, 1), (1, 1))))
    tissue_rim = jnp.pad(tissue, ((0, 0), (1, 1), (1, 1)))
    displace = start_field
    for sweep in range(ITERS):
        pulled = attract(displace, slopes, fixed_image, moving_slab, tissue)
        displace = smooth(jnp.pad(pulled, ((0, 0), (0, 0), (1, 1), (1, 1))), tissue_rim)
    return displace
```

```python
import jax
import jax.numpy as jnp
from jax import lax
from jax.experimental import pallas as pl
from jax.experimental.pallas import tpu as pltpu
from jax.sharding import PartitionSpec as P

ITERS = 3
pull_rate = 1.0
smooth_rate = 0.16

NZ = 32
BY = 16
HY = 8
RY = BY + HY
LX = 128
EX = LX // NZ
ZG = 8

VMEM = pltpu.VMEM
f32 = jnp.float32


def iota(shape, dim):
    return lax.broadcasted_iota(jnp.int32, shape, dim)


def cut_kernel(slab_ref, out_ref):
    count = slab_ref.shape[0]
    low = iota((HY, LX), 0) < HY // 2
    zero = jnp.zeros((HY, LX), f32)
    for i in range(count):
        after = slab_ref[i + 1, 0:HY] if i + 1 < count else zero
        before = slab_ref[i - 1, HY:BY] if i else zero
        out_ref[i, 0:BY] = slab_ref[i]
        out_ref[i, BY:RY] = jnp.where(low, after, before)


def cut(slab):
    count = slab.shape[1] // BY
    return pl.pallas_call(
        cut_kernel,
        out_shape=jax.ShapeDtypeStruct((count, RY, LX), f32),
        in_specs=[pl.BlockSpec(memory_space=VMEM)],
        out_specs=pl.BlockSpec(memory_space=VMEM),
        name="cut",
    )(slab.reshape(count, BY, LX))


def pack_kernel(moving_ref, fixed_ref, field_ref, halo_ref, left_ref, right_ref):
    group = iota((RY, LX), 1) // EX

    def rows(which, z):
        if which == 4:
            return moving_ref[z]
        core = fixed_ref[z] if which == 3 else field_ref[which, z]
        return jnp.concatenate([core, halo_ref[which, z]], axis=0)

    for which in range(5):

        def step(z, packs):
            left, right = packs
            turned = pltpu.roll(rows(which, z), 4 * z + 4, 1)
            right = jnp.where(group == z, turned, right)
            left = jnp.where(group == lax.rem(z + 1, NZ), turned, left)
            return left, right

        zero = jnp.zeros((RY, LX), f32)
        left, right = lax.fori_loop(0, NZ, step, (zero, zero), unroll=4)
        left_ref[which] = pltpu.roll(left, LX - EX, 1)
        right_ref[which] = right


def pack(moving, fixed, field, halo):
    shape = jax.ShapeDtypeStruct((5, RY, LX), f32)
    return pl.pallas_call(
        pack_kernel,
        out_shape=(shape, shape),
        in_specs=[pl.BlockSpec(memory_space=VMEM)] * 4,
        out_specs=(pl.BlockSpec(memory_space=VMEM),) * 2,
        name="pack",
    )(moving, fixed, field, halo)


def recip(x):
    r = pl.reciprocal(x, approx=True)
    return r * (2.0 - x * r)


def attract(field, slopes, gap, energy, tissue):
    residual = gap - (slopes[0] * field[0] + slopes[1] * field[1] + slopes[2] * field[2])
    rate = pull_rate * tissue * residual * recip(energy + residual * residual)
    return [field[c] + rate * slopes[c] for c in range(3)]


def strip_neighbours(packs):
    lane = iota((RY, LX), 1)
    j = lane % EX
    first, last = j == 0, j == EX - 1
    low, high = lane < EX, lane >= LX - EX
    out = []
    for inner, pair in ((0, (0, 1)), (1, (0, 1)), (0, (2, 3)), (1, (2, 3))):
        a, b = packs[pair[0]], packs[pair[1]]
        own = b if inner else a
        before = jnp.where(first, pltpu.roll(a, LX - EX + 1, 1), pltpu.roll(b, 1, 1)) if inner else pltpu.roll(a, 1, 1)
        after = pltpu.roll(b, LX - 1, 1) if inner else jnp.where(last, pltpu.roll(b, EX - 1, 1), pltpu.roll(a, LX - 1, 1))
        out.append(
            (
                jnp.where(high, 0.0, pltpu.roll(own, LX - EX, 1)),
                jnp.where(low, 0.0, pltpu.roll(own, EX, 1)),
                pltpu.roll(own, RY - 1, 0),
                pltpu.roll(own, 1, 0),
                after,
                before,
            )
        )
    return out


def beside(packs):
    j = iota((RY, LX), 1) % EX
    return jnp.where(j == 2, pltpu.roll(packs[0], LX - 1, 1), pltpu.roll(packs[3], 1, 1))


def total(neighbours):
    up, down, after_y, before_y, after_x, before_x = neighbours
    return ((up + down) + (after_y + before_y)) + (after_x + before_x)


def main_kernel(
    tissue_ref,
    inside_ref,
    moving_ref,
    fixed_ref,
    field_ref,
    halo_ref,
    own_left_ref,
    own_right_ref,
    got_left_ref,
    got_right_ref,
    out_ref,
    slope_ref,
    energy_ref,
    gap_ref,
    ping_ref,
    pong_ref,
    beside_ref,
    tissue_rows_ref,
    keep_ref,
):
    lane = iota((RY, LX), 1)
    row = iota((RY, LX), 0)
    at_left, at_right = lane == 0, lane == LX - 1
    groups = NZ // ZG

    def rows_of(column, group):
        def at(k):
            return tissue_ref[(group * 3 + k) * 3 + column]

        return jnp.where(row < BY, at(1), jnp.where(row < BY + HY // 2, at(2), at(0)))

    cells = [rows_of(1, g) for g in range(groups)]
    flat = []
    for g in range(groups):
        own = cells[g]
        tissue_rows_ref[g] = own
        across = jnp.where(at_left, rows_of(0, g), own) + jnp.where(at_right, rows_of(2, g), own)
        flat.append(across + pltpu.roll(own, 1, 0) + pltpu.roll(own, RY - 1, 0))
    zero = jnp.zeros((RY, LX), f32)
    for g in range(groups):
        below = cells[g - 1] if g else zero
        above = cells[g + 1] if g + 1 < groups else zero
        keep_ref[3 * g] = 1.0 - smooth_rate * cells[g] * (flat[g] + below + cells[g])
        keep_ref[3 * g + 1] = 1.0 - smooth_rate * cells[g] * (flat[g] + cells[g] + cells[g])
        keep_ref[3 * g + 2] = 1.0 - smooth_rate * cells[g] * (flat[g] + cells[g] + above)

    def strips(which, edge=None):
        a, d = got_left_ref[which], got_right_ref[which]
        if edge is not None:
            a, d = a * edge[0], d * edge[1]
        return [a, own_left_ref[which], own_right_ref[which], d]

    strip_tissue = []
    for column in (0, 1, 1, 2):
        cell = rows_of(column, groups - 1)
        for g in range(groups - 2, -1, -1):
            cell = jnp.where(lane < (g + 1) * ZG * EX, rows_of(column, g), cell)
        strip_tissue.append(cell)
    strip_keep = [
        1.0 - smooth_rate * t * total(n) for t, n in zip(strip_tissue, strip_neighbours(strip_tissue))
    ]
    strip_moving = strips(4, (inside_ref[0], inside_ref[1]))
    strip_slopes, strip_energy = [], []
    for up, down, after_y, before_y, after_x, before_x in strip_neighbours(strip_moving):
        s = [0.5 * (up - down), 0.5 * (after_y - before_y), 0.5 * (after_x - before_x)]
        strip_slopes.append(s)
        strip_energy.append(s[0] * s[0] + s[1] * s[1] + s[2] * s[2] + 0.5)
    strip_gap = [f - m for f, m in zip(strips(3), strip_moving)]
    strip_field = [[x * t for x, t in zip(strips(c), strip_tissue)] for c in range(3)]

    def strip_attract():
        parts = [
            attract([strip_field[c][k] for c in range(3)], strip_slopes[k], strip_gap[k], strip_energy[k], strip_tissue[k])
            for k in range(4)
        ]
        return [[parts[k][c] for k in range(4)] for c in range(3)]

    def strip_smooth(pulled):
        out = []
        for c in range(3):
            near = strip_neighbours(pulled[c])
            out.append(
                [strip_keep[k] * pulled[c][k] + smooth_rate * strip_tissue[k] * total(near[k]) for k in range(4)]
            )
        return out

    def edges(values, side, rows=RY):
        before = jnp.where(at_left[:rows], side, pltpu.roll(values, 1, 1))
        after = jnp.where(at_right[:rows], side, pltpu.roll(values, LX - 1, 1))
        return before, after

    def side_at(c, z):
        return pltpu.roll(beside_ref[c], LX - 2 - EX * z, 1)

    beside_ref[0] = beside(strip_moving)
    for ref in (ping_ref, pong_ref):
        for c in range(3):
            ref[c, 0] = zero
            ref[c, NZ + 1] = zero

    def first(z, carry):
        m = moving_ref[z]
        above = jnp.where(z < NZ - 1, moving_ref[jnp.minimum(z + 1, NZ - 1)], 0.0)
        below = jnp.where(z > 0, moving_ref[jnp.maximum(z - 1, 0)], 0.0)
        before, after = edges(m, side_at(0, z))
        s = [
            0.5 * (above - below),
            0.5 * (pltpu.roll(m, RY - 1, 0) - pltpu.roll(m, 1, 0)),
            0.5 * (after - before),
        ]
        energy = s[0] * s[0] + s[1] * s[1] + s[2] * s[2] + 0.5
        gap = jnp.concatenate([fixed_ref[z], halo_ref[3, z]], axis=0) - m
        t = tissue_rows_ref[z // ZG]
        field = [t * jnp.concatenate([field_ref[c, z], halo_ref[c, z]], axis=0) for c in range(3)]
        pulled = attract(field, s, gap, energy, t)
        for c in range(3):
            slope_ref[c, z] = s[c]
            ping_ref[c, z + 1] = pulled[c]
        energy_ref[z] = energy
        gap_ref[z] = gap
        return carry

    lax.fori_loop(0, NZ, first, 0, unroll=2)

    def smoothed(src, z, c, t, keep, rows):
        p = src[c, z + 1]
        before, after = edges(p[:rows], side_at(c, z)[:rows], rows)
        y = pltpu.roll(p, RY - 1, 0) + pltpu.roll(p, 1, 0)
        around = ((src[c, z + 2][:rows] + src[c, z][:rows]) + y[:rows]) + (before + after)
        return keep * p[:rows] + (smooth_rate * t) * around

    def keep_at(z):
        g, k = z // ZG, z % ZG
        return keep_ref[3 * g + jnp.where(k == 0, 0, jnp.where(k == ZG - 1, 2, 1))]

    src, dst = ping_ref, pong_ref
    for sweep in range(ITERS):
        pulled = strip_attract()
        for c in range(3):
            beside_ref[c] = beside(pulled[c])
        if sweep < ITERS - 1:
            strip_field = strip_smooth(pulled)

            def middle(z, carry, src=src, dst=dst):
                t = tissue_rows_ref[z // ZG]
                keep = keep_at(z)
                field = [smoothed(src, z, c, t, keep, RY) for c in range(3)]
                s = [slope_ref[c, z] for c in range(3)]
                pulled = attract(field, s, gap_ref[z], energy_ref[z], t)
                for c in range(3):
                    dst[c, z + 1] = pulled[c]
                return carry

            lax.fori_loop(0, NZ, middle, 0, unroll=2)
            src, dst = dst, src
        else:

            def final(z, carry, src=src):
                t = tissue_rows_ref[z // ZG][:BY]
                keep = keep_at(z)[:BY]
                for c in range(3):
                    out_ref[c, z] = smoothed(src, z, c, t, keep, BY)
                return carry

            lax.fori_loop(0, NZ, final, 0, unroll=2)


def register(tissue, inside, moving, fixed, field, halo, own_left, own_right, got_left, got_right):
    smem = pl.BlockSpec(memory_space=pltpu.SMEM)
    vmem = pl.BlockSpec(memory_space=VMEM)
    return pl.pallas_call(
        main_kernel,
        out_shape=jax.ShapeDtypeStruct((3, NZ, BY, LX), f32),
        in_specs=[smem, smem] + [vmem] * 8,
        out_specs=vmem,
        scratch_shapes=[
            VMEM((3, NZ, RY, LX), f32),
            VMEM((NZ, RY, LX), f32),
            VMEM((NZ, RY, LX), f32),
            VMEM((3, NZ + 2, RY, LX), f32),
            VMEM((3, NZ + 2, RY, LX), f32),
            VMEM((3, RY, LX), f32),
            VMEM((NZ // ZG, RY, LX), f32),
            VMEM((3 * NZ // ZG, RY, LX), f32),
        ],
        compiler_params=pltpu.CompilerParams(vmem_limit_bytes=24 * 2**20),
        name="register",
    )(tissue, inside, moving, fixed, field, halo, own_left, own_right, got_left, got_right)


def turn(x, axis, by):
    size = lax.axis_size(axis)
    return lax.ppermute(x, axis, [(i, (i + by) % size) for i in range(size)])


def body(moving_slab, fixed_image, start_field, tissue_mask):
    row = lax.axis_index("row")
    col = lax.axis_index("col")
    blocks = cut(moving_slab)
    moving = lax.all_to_all(blocks, "row", split_axis=0, concat_axis=0, tiled=True)

    state = jnp.concatenate([start_field, fixed_image[None]], axis=0)
    after = turn(state[:, :, 0 : HY // 2], "row", -1)
    before = turn(state[:, :, BY - HY // 2 :], "row", 1)
    halo = jnp.concatenate([after, before], axis=2)

    padded = jnp.pad(tissue_mask, ((0, 0), (1, 1), (1, 1))).astype(f32)
    tissue = lax.dynamic_slice(padded, (0, row, col), (NZ // ZG, 3, 3)).reshape(-1)
    inside = jnp.stack([col > 0, col < lax.axis_size("col") - 1]).astype(f32)

    own_left, own_right = pack(moving, fixed_image, start_field, halo)
    got_left = turn(own_right, "col", 1)
    got_right = turn(own_left, "col", -1)
    return register(
        tissue, inside, moving, fixed_image, start_field, halo, own_left, own_right, got_left, got_right
    )


def solution(mesh):
    in_specs = (P("row", None, "col"), P(None, "row", "col"), P(None, None, "row", "col"), P())
    out_specs = P(None, None, "row", "col")
    return jax.shard_map(body, mesh=mesh, in_specs=in_specs, out_specs=out_specs, check_vma=False)
```

```python
import jax
import jax.numpy as jnp
from jax import lax
from jax.experimental import pallas as pl
from jax.experimental.pallas import tpu as pltpu
from jax.sharding import PartitionSpec as P

ITERS = 3
pull_rate = 1.0
smooth_rate = 0.16

NZ = 32
BY = 16
HY = 8
RY = BY + HY
LX = 128
EX = LX // NZ
ZG = 8

VMEM = pltpu.VMEM
f32 = jnp.float32


def iota(shape, dim):
    return lax.broadcasted_iota(jnp.int32, shape, dim)


def cut_kernel(slab_ref, out_ref):
    count = slab_ref.shape[0]
    low = iota((HY, LX), 0) < HY // 2
    zero = jnp.zeros((HY, LX), f32)
    for i in range(count):
        after = slab_ref[i + 1, 0:HY] if i + 1 < count else zero
        before = slab_ref[i - 1, HY:BY] if i else zero
        out_ref[i, 0:BY] = slab_ref[i]
        out_ref[i, BY:RY] = jnp.where(low, after, before)


def cut(slab):
    count = slab.shape[1] // BY
    return pl.pallas_call(
        cut_kernel,
        out_shape=jax.ShapeDtypeStruct((count, RY, LX), f32),
        in_specs=[pl.BlockSpec(memory_space=VMEM)],
        out_specs=pl.BlockSpec(memory_space=VMEM),
        compiler_params=pltpu.CompilerParams(vmem_limit_bytes=4 * 2**20),
        name="cut",
    )(slab.reshape(count, BY, LX))


def pack_kernel(moving_ref, fixed_ref, field_ref, halo_ref, left_ref, right_ref):
    group = iota((RY, LX), 1) // EX

    def rows(which, z):
        if which == 4:
            return moving_ref[z]
        core = fixed_ref[z] if which == 3 else field_ref[which, z]
        return jnp.concatenate([core, halo_ref[which, z]], axis=0)

    for which in range(5):

        def step(z, packs):
            left, right = packs
            turned = pltpu.roll(rows(which, z), 4 * z + 4, 1)
            right = jnp.where(group == z, turned, right)
            left = jnp.where(group == lax.rem(z + 1, NZ), turned, left)
            return left, right

        zero = jnp.zeros((RY, LX), f32)
        left, right = lax.fori_loop(0, NZ, step, (zero, zero), unroll=NZ)
        left_ref[which] = pltpu.roll(left, LX - EX, 1)
        right_ref[which] = right


def pack(moving, fixed, field, halo):
    shape = jax.ShapeDtypeStruct((5, RY, LX), f32)
    return pl.pallas_call(
        pack_kernel,
        out_shape=(shape, shape),
        in_specs=[pl.BlockSpec(memory_space=VMEM)] * 4,
        out_specs=(pl.BlockSpec(memory_space=VMEM),) * 2,
        compiler_params=pltpu.CompilerParams(vmem_limit_bytes=8 * 2**20),
        name="pack",
    )(moving, fixed, field, halo)


def recip(x):
    r = pl.reciprocal(x, approx=True)
    return r * (2.0 - x * r)


def attract(field, slopes, gap, energy, tissue):
    residual = gap - (slopes[0] * field[0] + slopes[1] * field[1] + slopes[2] * field[2])
    rate = pull_rate * tissue * residual * recip(energy + residual * residual)
    return [field[c] + rate * slopes[c] for c in range(3)]


def strip_neighbours(packs):
    lane = iota((RY, LX), 1)
    j = lane % EX
    first, last = j == 0, j == EX - 1
    low, high = lane < EX, lane >= LX - EX
    out = []
    for inner, pair in ((0, (0, 1)), (1, (0, 1)), (0, (2, 3)), (1, (2, 3))):
        a, b = packs[pair[0]], packs[pair[1]]
        own = b if inner else a
        before = jnp.where(first, pltpu.roll(a, LX - EX + 1, 1), pltpu.roll(b, 1, 1)) if inner else pltpu.roll(a, 1, 1)
        after = pltpu.roll(b, LX - 1, 1) if inner else jnp.where(last, pltpu.roll(b, EX - 1, 1), pltpu.roll(a, LX - 1, 1))
        out.append(
            (
                jnp.where(high, 0.0, pltpu.roll(own, LX - EX, 1)),
                jnp.where(low, 0.0, pltpu.roll(own, EX, 1)),
                pltpu.roll(own, RY - 1, 0),
                pltpu.roll(own, 1, 0),
                after,
                before,
            )
        )
    return out


def beside(packs):
    j = iota((RY, LX), 1) % EX
    return jnp.where(j == 2, pltpu.roll(packs[0], LX - 1, 1), pltpu.roll(packs[3], 1, 1))


def total(neighbours):
    up, down, after_y, before_y, after_x, before_x = neighbours
    return ((up + down) + (after_y + before_y)) + (after_x + before_x)


def main_kernel(
    tissue_ref,
    inside_ref,
    moving_ref,
    fixed_ref,
    field_ref,
    halo_ref,
    own_left_ref,
    own_right_ref,
    got_left_ref,
    got_right_ref,
    out_ref,
    slope_ref,
    energy_ref,
    gap_ref,
    ping_ref,
    pong_ref,
    beside_ref,
    tissue_rows_ref,
    keep_ref,
):
    lane = iota((RY, LX), 1)
    row = iota((RY, LX), 0)
    at_left, at_right = lane == 0, lane == LX - 1
    groups = NZ // ZG

    def rows_of(column, group):
        def at(k):
            return tissue_ref[(group * 3 + k) * 3 + column]

        return jnp.where(row < BY, at(1), jnp.where(row < BY + HY // 2, at(2), at(0)))

    cells = [rows_of(1, g) for g in range(groups)]
    flat = []
    for g in range(groups):
        own = cells[g]
        tissue_rows_ref[g] = own
        across = jnp.where(at_left, rows_of(0, g), own) + jnp.where(at_right, rows_of(2, g), own)
        flat.append(across + pltpu.roll(own, 1, 0) + pltpu.roll(own, RY - 1, 0))
    zero = jnp.zeros((RY, LX), f32)
    for g in range(groups):
        below = cells[g - 1] if g else zero
        above = cells[g + 1] if g + 1 < groups else zero
        keep_ref[3 * g] = 1.0 - smooth_rate * cells[g] * (flat[g] + below + cells[g])
        keep_ref[3 * g + 1] = 1.0 - smooth_rate * cells[g] * (flat[g] + cells[g] + cells[g])
        keep_ref[3 * g + 2] = 1.0 - smooth_rate * cells[g] * (flat[g] + cells[g] + above)

    def strips(which, edge=None):
        a, d = got_left_ref[which], got_right_ref[which]
        if edge is not None:
            a, d = a * edge[0], d * edge[1]
        return [a, own_left_ref[which], own_right_ref[which], d]

    strip_tissue = []
    for column in (0, 1, 1, 2):
        cell = rows_of(column, groups - 1)
        for g in range(groups - 2, -1, -1):
            cell = jnp.where(lane < (g + 1) * ZG * EX, rows_of(column, g), cell)
        strip_tissue.append(cell)
    strip_keep = [
        1.0 - smooth_rate * t * total(n) for t, n in zip(strip_tissue, strip_neighbours(strip_tissue))
    ]
    strip_moving = strips(4, (inside_ref[0], inside_ref[1]))
    strip_slopes, strip_energy = [], []
    for up, down, after_y, before_y, after_x, before_x in strip_neighbours(strip_moving):
        s = [0.5 * (up - down), 0.5 * (after_y - before_y), 0.5 * (after_x - before_x)]
        strip_slopes.append(s)
        strip_energy.append(s[0] * s[0] + s[1] * s[1] + s[2] * s[2] + 0.5)
    strip_gap = [f - m for f, m in zip(strips(3), strip_moving)]
    strip_field = [[x * t for x, t in zip(strips(c), strip_tissue)] for c in range(3)]

    def strip_attract():
        parts = [
            attract([strip_field[c][k] for c in range(3)], strip_slopes[k], strip_gap[k], strip_energy[k], strip_tissue[k])
            for k in range(4)
        ]
        return [[parts[k][c] for k in range(4)] for c in range(3)]

    def strip_smooth(pulled):
        out = []
        for c in range(3):
            near = strip_neighbours(pulled[c])
            out.append(
                [strip_keep[k] * pulled[c][k] + smooth_rate * strip_tissue[k] * total(near[k]) for k in range(4)]
            )
        return out

    def edges(values, side, rows=RY):
        before = jnp.where(at_left[:rows], side, pltpu.roll(values, 1, 1))
        after = jnp.where(at_right[:rows], side, pltpu.roll(values, LX - 1, 1))
        return before, after

    def side_at(c, z):
        return pltpu.roll(beside_ref[c], LX - 2 - EX * z, 1)

    beside_ref[0] = beside(strip_moving)
    for ref in (ping_ref, pong_ref):
        for c in range(3):
            ref[c, 0] = zero
            ref[c, NZ + 1] = zero

    def first(z, carry):
        m = moving_ref[z]
        above = jnp.where(z < NZ - 1, moving_ref[jnp.minimum(z + 1, NZ - 1)], 0.0)
        below = jnp.where(z > 0, moving_ref[jnp.maximum(z - 1, 0)], 0.0)
        before, after = edges(m, side_at(0, z))
        s = [
            0.5 * (above - below),
            0.5 * (pltpu.roll(m, RY - 1, 0) - pltpu.roll(m, 1, 0)),
            0.5 * (after - before),
        ]
        energy = s[0] * s[0] + s[1] * s[1] + s[2] * s[2] + 0.5
        gap = jnp.concatenate([fixed_ref[z], halo_ref[3, z]], axis=0) - m
        t = tissue_rows_ref[z // ZG]
        field = [t * jnp.concatenate([field_ref[c, z], halo_ref[c, z]], axis=0) for c in range(3)]
        pulled = attract(field, s, gap, energy, t)
        for c in range(3):
            slope_ref[c, z] = s[c]
            ping_ref[c, z + 1] = pulled[c]
        energy_ref[z] = energy
        gap_ref[z] = gap
        return carry

    lax.fori_loop(0, NZ, first, 0, unroll=NZ)

    def smoothed(src, z, c, t, keep, rows):
        p = src[c, z + 1]
        before, after = edges(p[:rows], side_at(c, z)[:rows], rows)
        y = pltpu.roll(p, RY - 1, 0) + pltpu.roll(p, 1, 0)
        around = ((src[c, z + 2][:rows] + src[c, z][:rows]) + y[:rows]) + (before + after)
        return keep * p[:rows] + (smooth_rate * t) * around

    def keep_at(z):
        g, k = z // ZG, z % ZG
        return keep_ref[3 * g + jnp.where(k == 0, 0, jnp.where(k == ZG - 1, 2, 1))]

    src, dst = ping_ref, pong_ref
    for sweep in range(ITERS):
        pulled = strip_attract()
        for c in range(3):
            beside_ref[c] = beside(pulled[c])
        if sweep < ITERS - 1:
            strip_field = strip_smooth(pulled)

            def middle(z, carry, src=src, dst=dst):
                t = tissue_rows_ref[z // ZG]
                keep = keep_at(z)
                field = [smoothed(src, z, c, t, keep, RY) for c in range(3)]
                s = [slope_ref[c, z] for c in range(3)]
                pulled = attract(field, s, gap_ref[z], energy_ref[z], t)
                for c in range(3):
                    dst[c, z + 1] = pulled[c]
                return carry

            lax.fori_loop(0, NZ, middle, 0, unroll=NZ)
            src, dst = dst, src
        else:

            def final(z, carry, src=src):
                t = tissue_rows_ref[z // ZG][:BY]
                keep = keep_at(z)[:BY]
                for c in range(3):
                    out_ref[c, z] = smoothed(src, z, c, t, keep, BY)
                return carry

            lax.fori_loop(0, NZ, final, 0, unroll=NZ)


def register(tissue, inside, moving, fixed, field, halo, own_left, own_right, got_left, got_right):
    smem = pl.BlockSpec(memory_space=pltpu.SMEM)
    vmem = pl.BlockSpec(memory_space=VMEM)
    return pl.pallas_call(
        main_kernel,
        out_shape=jax.ShapeDtypeStruct((3, NZ, BY, LX), f32),
        in_specs=[smem, smem] + [vmem] * 8,
        out_specs=vmem,
        scratch_shapes=[
            VMEM((3, NZ, RY, LX), f32),
            VMEM((NZ, RY, LX), f32),
            VMEM((NZ, RY, LX), f32),
            VMEM((3, NZ + 2, RY, LX), f32),
            VMEM((3, NZ + 2, RY, LX), f32),
            VMEM((3, RY, LX), f32),
            VMEM((NZ // ZG, RY, LX), f32),
            VMEM((3 * NZ // ZG, RY, LX), f32),
        ],
        compiler_params=pltpu.CompilerParams(vmem_limit_bytes=16 * 2**20),
        name="register",
    )(tissue, inside, moving, fixed, field, halo, own_left, own_right, got_left, got_right)


def turn(x, axis, by):
    size = lax.axis_size(axis)
    return lax.ppermute(x, axis, [(i, (i + by) % size) for i in range(size)])


def body(moving_slab, fixed_image, start_field, tissue_mask):
    row = lax.axis_index("row")
    col = lax.axis_index("col")
    blocks = cut(moving_slab)
    moving = lax.all_to_all(blocks, "row", split_axis=0, concat_axis=0, tiled=True)

    state = jnp.concatenate([start_field, fixed_image[None]], axis=0)
    after = turn(state[:, :, 0 : HY // 2], "row", -1)
    before = turn(state[:, :, BY - HY // 2 :], "row", 1)
    halo = jnp.concatenate([after, before], axis=2)

    padded = jnp.pad(tissue_mask, ((0, 0), (1, 1), (1, 1))).astype(f32)
    tissue = lax.dynamic_slice(padded, (0, row, col), (NZ // ZG, 3, 3)).reshape(-1)
    inside = jnp.stack([col > 0, col < lax.axis_size("col") - 1]).astype(f32)

    own_left, own_right = pack(moving, fixed_image, start_field, halo)
    got_left = turn(own_right, "col", 1)
    got_right = turn(own_left, "col", -1)
    return register(
        tissue, inside, moving, fixed_image, start_field, halo, own_left, own_right, got_left, got_right
    )


def solution(mesh):
    in_specs = (P("row", None, "col"), P(None, "row", "col"), P(None, None, "row", "col"), P())
    out_specs = P(None, None, "row", "col")
    return jax.shard_map(body, mesh=mesh, in_specs=in_specs, out_specs=out_specs, check_vma=False)
```

```python
import jax
import jax.numpy as jnp
from jax import lax
from jax.experimental import pallas as pl
from jax.experimental.pallas import tpu as pltpu
from jax.sharding import PartitionSpec as P

ITERS = 3
pull_rate = 1.0
smooth_rate = 0.16

NZ = 32
BY = 16
HY = 8
RY = BY + HY
LX = 128
EX = LX // NZ
ZG = 8

VMEM = pltpu.VMEM
f32 = jnp.float32


def iota(shape, dim):
    return lax.broadcasted_iota(jnp.int32, shape, dim)


def cut_kernel(slab_ref, out_ref):
    count = slab_ref.shape[0]
    low = iota((HY, LX), 0) < HY // 2
    zero = jnp.zeros((HY, LX), f32)
    for i in range(count):
        after = slab_ref[i + 1, 0:HY] if i + 1 < count else zero
        before = slab_ref[i - 1, HY:BY] if i else zero
        out_ref[i, 0:BY] = slab_ref[i]
        out_ref[i, BY:RY] = jnp.where(low, after, before)


def cut(slab):
    count = slab.shape[1] // BY
    return pl.pallas_call(
        cut_kernel,
        out_shape=jax.ShapeDtypeStruct((count, RY, LX), f32),
        in_specs=[pl.BlockSpec(memory_space=VMEM)],
        out_specs=pl.BlockSpec(memory_space=VMEM),
        compiler_params=pltpu.CompilerParams(vmem_limit_bytes=4 * 2**20),
        name="cut",
    )(slab.reshape(count, BY, LX))


def halo_rows(after_ref, before_ref, which, z):
    return [after_ref[which, z], before_ref[which, z]]


def pack_rows(rows, left_ref, right_ref, which):
    group = iota((RY, LX), 1) // EX
    left = right = jnp.zeros((RY, LX), f32)
    for z in range(NZ):
        turned = pltpu.roll(rows(z), (EX * (z + 1)) % LX, 1)
        right = jnp.where(group == z, turned, right)
        left = jnp.where(group == (z + 1) % NZ, turned, left)
    left_ref[which] = pltpu.roll(left, LX - EX, 1)
    right_ref[which] = right


def pack_state_kernel(fixed_ref, field_ref, after_ref, before_ref, left_ref, right_ref):
    for which in range(4):

        def rows(z):
            core = fixed_ref[z] if which == 3 else field_ref[which, z]
            return jnp.concatenate([core] + halo_rows(after_ref, before_ref, which, z), axis=0)

        pack_rows(rows, left_ref, right_ref, which)


def pack_moving_kernel(moving_ref, left_in_ref, right_in_ref, left_ref, right_ref):
    del left_in_ref, right_in_ref
    pack_rows(lambda z: moving_ref[z], left_ref, right_ref, 4)


def pack(moving, fixed, field, after, before):
    shape = jax.ShapeDtypeStruct((5, RY, LX), f32)
    vmem = pl.BlockSpec(memory_space=VMEM)
    packs = pl.pallas_call(
        pack_state_kernel,
        out_shape=(shape, shape),
        in_specs=[vmem] * 4,
        out_specs=(vmem, vmem),
        compiler_params=pltpu.CompilerParams(vmem_limit_bytes=8 * 2**20),
        cost_estimate=pl.CostEstimate(flops=20000000000, bytes_accessed=2**20, transcendentals=0),
        name="pack_state",
    )(fixed, field, after, before)
    return pl.pallas_call(
        pack_moving_kernel,
        out_shape=(shape, shape),
        in_specs=[vmem] * 3,
        out_specs=(vmem, vmem),
        input_output_aliases={1: 0, 2: 1},
        compiler_params=pltpu.CompilerParams(vmem_limit_bytes=4 * 2**20),
        name="pack_moving",
    )(moving, *packs)


def recip(x):
    r = pl.reciprocal(x, approx=True)
    return r * (2.0 - x * r)


def attract(field, slopes, gap, energy, tissue):
    residual = gap - (slopes[0] * field[0] + slopes[1] * field[1] + slopes[2] * field[2])
    rate = pull_rate * tissue * residual * recip(energy + residual * residual)
    return [field[c] + rate * slopes[c] for c in range(3)]


def strip_neighbours(packs):
    lane = iota((RY, LX), 1)
    j = lane % EX
    first, last = j == 0, j == EX - 1
    low, high = lane < EX, lane >= LX - EX
    out = []
    for inner, pair in ((0, (0, 1)), (1, (0, 1)), (0, (2, 3)), (1, (2, 3))):
        a, b = packs[pair[0]], packs[pair[1]]
        own = b if inner else a
        before = jnp.where(first, pltpu.roll(a, LX - EX + 1, 1), pltpu.roll(b, 1, 1)) if inner else pltpu.roll(a, 1, 1)
        after = pltpu.roll(b, LX - 1, 1) if inner else jnp.where(last, pltpu.roll(b, EX - 1, 1), pltpu.roll(a, LX - 1, 1))
        out.append(
            (
                jnp.where(high, 0.0, pltpu.roll(own, LX - EX, 1)),
                jnp.where(low, 0.0, pltpu.roll(own, EX, 1)),
                pltpu.roll(own, RY - 1, 0),
                pltpu.roll(own, 1, 0),
                after,
                before,
            )
        )
    return out


def beside(packs):
    j = iota((RY, LX), 1) % EX
    return jnp.where(j == 2, pltpu.roll(packs[0], LX - 1, 1), pltpu.roll(packs[3], 1, 1))


def total(neighbours):
    up, down, after_y, before_y, after_x, before_x = neighbours
    return ((up + down) + (after_y + before_y)) + (after_x + before_x)


def main_kernel(
    tissue_ref,
    inside_ref,
    moving_ref,
    fixed_ref,
    field_ref,
    after_ref,
    before_ref,
    own_left_ref,
    own_right_ref,
    got_left_ref,
    got_right_ref,
    out_ref,
    slope_ref,
    energy_ref,
    gap_ref,
    ping_ref,
    pong_ref,
    beside_ref,
    tissue_rows_ref,
    keep_ref,
):
    lane = iota((RY, LX), 1)
    row = iota((RY, LX), 0)
    at_left, at_right = lane == 0, lane == LX - 1
    groups = NZ // ZG

    def rows_of(column, group):
        def at(k):
            return tissue_ref[(group * 3 + k) * 3 + column]

        return jnp.where(row < BY, at(1), jnp.where(row < BY + HY // 2, at(2), at(0)))

    cells = [rows_of(1, g) for g in range(groups)]
    flat = []
    for g in range(groups):
        own = cells[g]
        tissue_rows_ref[g] = own
        across = jnp.where(at_left, rows_of(0, g), own) + jnp.where(at_right, rows_of(2, g), own)
        flat.append(across + pltpu.roll(own, 1, 0) + pltpu.roll(own, RY - 1, 0))
    zero = jnp.zeros((RY, LX), f32)
    for g in range(groups):
        below = cells[g - 1] if g else zero
        above = cells[g + 1] if g + 1 < groups else zero
        keep_ref[3 * g] = 1.0 - smooth_rate * cells[g] * (flat[g] + below + cells[g])
        keep_ref[3 * g + 1] = 1.0 - smooth_rate * cells[g] * (flat[g] + cells[g] + cells[g])
        keep_ref[3 * g + 2] = 1.0 - smooth_rate * cells[g] * (flat[g] + cells[g] + above)

    def strips(which, edge=None):
        a, d = got_left_ref[which], got_right_ref[which]
        if edge is not None:
            a, d = a * edge[0], d * edge[1]
        return [a, own_left_ref[which], own_right_ref[which], d]

    strip_tissue = []
    for column in (0, 1, 1, 2):
        cell = rows_of(column, groups - 1)
        for g in range(groups - 2, -1, -1):
            cell = jnp.where(lane < (g + 1) * ZG * EX, rows_of(column, g), cell)
        strip_tissue.append(cell)
    strip_keep = [
        1.0 - smooth_rate * t * total(n) for t, n in zip(strip_tissue, strip_neighbours(strip_tissue))
    ]
    strip_moving = strips(4, (inside_ref[0], inside_ref[1]))
    strip_slopes, strip_energy = [], []
    for up, down, after_y, before_y, after_x, before_x in strip_neighbours(strip_moving):
        s = [0.5 * (up - down), 0.5 * (after_y - before_y), 0.5 * (after_x - before_x)]
        strip_slopes.append(s)
        strip_energy.append(s[0] * s[0] + s[1] * s[1] + s[2] * s[2] + 0.5)
    strip_gap = [f - m for f, m in zip(strips(3), strip_moving)]
    strip_field = [[x * t for x, t in zip(strips(c), strip_tissue)] for c in range(3)]

    def strip_attract():
        parts = [
            attract([strip_field[c][k] for c in range(3)], strip_slopes[k], strip_gap[k], strip_energy[k], strip_tissue[k])
            for k in range(4)
        ]
        return [[parts[k][c] for k in range(4)] for c in range(3)]

    def strip_smooth(pulled):
        out = []
        for c in range(3):
            near = strip_neighbours(pulled[c])
            out.append(
                [strip_keep[k] * pulled[c][k] + smooth_rate * strip_tissue[k] * total(near[k]) for k in range(4)]
            )
        return out

    def edges(values, side, rows=RY):
        before = jnp.where(at_left[:rows], side, pltpu.roll(values, 1, 1))
        after = jnp.where(at_right[:rows], side, pltpu.roll(values, LX - 1, 1))
        return before, after

    def side_at(c, z):
        return pltpu.roll(beside_ref[c], LX - 2 - EX * z, 1)

    beside_ref[0] = beside(strip_moving)
    for ref in (ping_ref, pong_ref):
        for c in range(3):
            ref[c, 0] = zero
            ref[c, NZ + 1] = zero

    def first(z, carry):
        m = moving_ref[z]
        above = jnp.where(z < NZ - 1, moving_ref[jnp.minimum(z + 1, NZ - 1)], 0.0)
        below = jnp.where(z > 0, moving_ref[jnp.maximum(z - 1, 0)], 0.0)
        before, after = edges(m, side_at(0, z))
        s = [
            0.5 * (above - below),
            0.5 * (pltpu.roll(m, RY - 1, 0) - pltpu.roll(m, 1, 0)),
            0.5 * (after - before),
        ]
        energy = s[0] * s[0] + s[1] * s[1] + s[2] * s[2] + 0.5
        gap = jnp.concatenate([fixed_ref[z]] + halo_rows(after_ref, before_ref, 3, z), axis=0) - m
        t = tissue_rows_ref[z // ZG]
        field = [
            t * jnp.concatenate([field_ref[c, z]] + halo_rows(after_ref, before_ref, c, z), axis=0) for c in range(3)
        ]
        pulled = attract(field, s, gap, energy, t)
        for c in range(3):
            slope_ref[c, z] = s[c]
            ping_ref[c, z + 1] = pulled[c]
        energy_ref[z] = energy
        gap_ref[z] = gap
        return carry

    lax.fori_loop(0, NZ, first, 0, unroll=NZ)

    def smoothed(src, z, c, t, keep, rows):
        p = src[c, z + 1]
        before, after = edges(p[:rows], side_at(c, z)[:rows], rows)
        y = pltpu.roll(p, RY - 1, 0) + pltpu.roll(p, 1, 0)
        around = ((src[c, z + 2][:rows] + src[c, z][:rows]) + y[:rows]) + (before + after)
        return keep * p[:rows] + (smooth_rate * t) * around

    def keep_at(z):
        g, k = z // ZG, z % ZG
        return keep_ref[3 * g + jnp.where(k == 0, 0, jnp.where(k == ZG - 1, 2, 1))]

    src, dst = ping_ref, pong_ref
    for sweep in range(ITERS):
        pulled = strip_attract()
        for c in range(3):
            beside_ref[c] = beside(pulled[c])
        if sweep < ITERS - 1:
            strip_field = strip_smooth(pulled)

            def middle(z, carry, src=src, dst=dst):
                t = tissue_rows_ref[z // ZG]
                keep = keep_at(z)
                field = [smoothed(src, z, c, t, keep, RY) for c in range(3)]
                s = [slope_ref[c, z] for c in range(3)]
                pulled = attract(field, s, gap_ref[z], energy_ref[z], t)
                for c in range(3):
                    dst[c, z + 1] = pulled[c]
                return carry

            lax.fori_loop(0, NZ, middle, 0, unroll=NZ)
            src, dst = dst, src
        else:

            def final(z, carry, src=src):
                t = tissue_rows_ref[z // ZG][:BY]
                keep = keep_at(z)[:BY]
                for c in range(3):
                    out_ref[c, z] = smoothed(src, z, c, t, keep, BY)
                return carry

            lax.fori_loop(0, NZ, final, 0, unroll=NZ)


def register(tissue, inside, moving, fixed, field, after, before, own_left, own_right, got_left, got_right):
    smem = pl.BlockSpec(memory_space=pltpu.SMEM)
    vmem = pl.BlockSpec(memory_space=VMEM)
    return pl.pallas_call(
        main_kernel,
        out_shape=jax.ShapeDtypeStruct((3, NZ, BY, LX), f32),
        in_specs=[smem, smem] + [vmem] * 9,
        out_specs=vmem,
        scratch_shapes=[
            VMEM((3, NZ, RY, LX), f32),
            VMEM((NZ, RY, LX), f32),
            VMEM((NZ, RY, LX), f32),
            VMEM((3, NZ + 2, RY, LX), f32),
            VMEM((3, NZ + 2, RY, LX), f32),
            VMEM((3, RY, LX), f32),
            VMEM((NZ // ZG, RY, LX), f32),
            VMEM((3 * NZ // ZG, RY, LX), f32),
        ],
        compiler_params=pltpu.CompilerParams(vmem_limit_bytes=16 * 2**20),
        name="register",
    )(tissue, inside, moving, fixed, field, after, before, own_left, own_right, got_left, got_right)


def turn(x, axis, by):
    size = lax.axis_size(axis)
    return lax.ppermute(x, axis, [(i, (i + by) % size) for i in range(size)])


def body(moving_slab, fixed_image, start_field, tissue_mask):
    row = lax.axis_index("row")
    col = lax.axis_index("col")
    blocks = cut(moving_slab)
    moving = lax.all_to_all(blocks, "row", split_axis=0, concat_axis=0, tiled=True)

    state = jnp.concatenate([start_field, fixed_image[None]], axis=0)
    after = turn(state[:, :, 0 : HY // 2], "row", -1)
    before = turn(state[:, :, BY - HY // 2 :], "row", 1)

    padded = jnp.pad(tissue_mask, ((0, 0), (1, 1), (1, 1))).astype(f32)
    tissue = lax.dynamic_slice(padded, (0, row, col), (NZ // ZG, 3, 3)).reshape(-1)
    inside = jnp.stack([col > 0, col < lax.axis_size("col") - 1]).astype(f32)

    own_left, own_right = pack(moving, fixed_image, start_field, after, before)
    got_left = turn(own_right, "col", 1)
    got_right = turn(own_left, "col", -1)
    return register(
        tissue, inside, moving, fixed_image, start_field, after, before, own_left, own_right, got_left, got_right
    )


def solution(mesh):
    in_specs = (P("row", None, "col"), P(None, "row", "col"), P(None, None, "row", "col"), P())
    out_specs = P(None, None, "row", "col")
    return jax.shard_map(body, mesh=mesh, in_specs=in_specs, out_specs=out_specs, check_vma=False)
```

```python
import jax
import jax.numpy as jnp
from jax import lax
from jax.experimental import pallas as pl
from jax.experimental.pallas import tpu as pltpu
from jax.sharding import PartitionSpec as P

ITERS = 3
pull_rate = 1.0
smooth_rate = 0.16

NZ = 32
BY = 16
HY = 8
RY = BY + HY
LX = 128
EX = LX // NZ
ZG = 8
GROUPS = NZ // ZG

VMEM = pltpu.VMEM
f32 = jnp.float32
vmem = pl.BlockSpec(memory_space=VMEM)
smem = pl.BlockSpec(memory_space=pltpu.SMEM)


def params(mib):
    return pltpu.CompilerParams(vmem_limit_bytes=mib * 2**20)


def iota(shape, dim):
    return lax.broadcasted_iota(jnp.int32, shape, dim)


def cut_kernel(slab_ref, out_ref):
    count = slab_ref.shape[0]
    low = iota((HY, LX), 0) < HY // 2
    zero = jnp.zeros((HY, LX), f32)
    for i in range(count):
        after = slab_ref[i + 1, 0:HY] if i + 1 < count else zero
        before = slab_ref[i - 1, HY:BY] if i else zero
        out_ref[i, 0:BY] = slab_ref[i]
        out_ref[i, BY:RY] = jnp.where(low, after, before)


def cut(slab):
    count = slab.shape[1] // BY
    return pl.pallas_call(
        cut_kernel,
        out_shape=jax.ShapeDtypeStruct((count, RY, LX), f32),
        in_specs=[vmem],
        out_specs=vmem,
        compiler_params=params(4),
        name="cut",
    )(slab.reshape(count, BY, LX))


def ring(core, after, before):
    return jnp.concatenate([core, after, before], axis=0)


def pack_rows(rows, refs, which):
    group = iota((RY, LX), 1) // EX
    packs = [jnp.zeros((RY, LX), f32)] * 4
    offsets = (1, 2, 0, -1)
    for z in range(NZ):
        turned = pltpu.roll(rows(z), (EX * (z + 1)) % LX, 1)
        packs = [jnp.where(group == (z + at) % NZ, turned, p) for at, p in zip(offsets, packs)]
    for at, p, ref in zip(offsets, packs, refs):
        ref[which] = pltpu.roll(p, (-EX * at) % LX, 1) if at else p


def pack_state_kernel(fixed_ref, field_ref, after_ref, before_ref, *refs):
    for which in range(4):

        def rows(z):
            core = fixed_ref[z] if which == 3 else field_ref[which, z]
            return ring(core, after_ref[which, z], before_ref[which, z])

        pack_rows(rows, refs, which)


def pack_moving_kernel(moving_ref, *refs):
    pack_rows(lambda z: moving_ref[z], refs[-4:], 4)


def pack(moving, fixed, field, after, before):
    shapes = (jax.ShapeDtypeStruct((5, RY, LX), f32),) * 4
    packs = pl.pallas_call(
        pack_state_kernel,
        out_shape=shapes,
        in_specs=[vmem] * 4,
        out_specs=(vmem,) * 4,
        compiler_params=params(8),
        cost_estimate=pl.CostEstimate(flops=20000000000, bytes_accessed=2**20, transcendentals=0),
        name="pack_state",
    )(fixed, field, after, before)
    return pl.pallas_call(
        pack_moving_kernel,
        out_shape=shapes,
        in_specs=[vmem] * 5,
        out_specs=(vmem,) * 4,
        input_output_aliases={1: 0, 2: 1, 3: 2, 4: 3},
        compiler_params=params(4),
        name="pack_moving",
    )(moving, *packs)


def recip(x):
    r = pl.reciprocal(x, approx=True)
    return r * (2.0 - x * r)


def energy_of(s):
    return s[0] * s[0] + s[1] * s[1] + s[2] * s[2] + 0.5


def attract(field, slopes, gap, energy, tissue):
    residual = gap - (slopes[0] * field[0] + slopes[1] * field[1] + slopes[2] * field[2])
    rate = pull_rate * tissue * residual * recip(energy + residual * residual)
    return [field[c] + rate * slopes[c] for c in range(3)]


def tissue_rows(tissue_ref, column, group):
    row = iota((RY, LX), 0)

    def at(k):
        return tissue_ref[(group * 3 + k) * 3 + column]

    return jnp.where(row < BY, at(1), jnp.where(row < BY + HY // 2, at(2), at(0)))


def core_kernel(
    tissue_ref,
    moving_ref,
    fixed_ref,
    field_ref,
    after_ref,
    before_ref,
    out_ref,
    slope_ref,
    energy_ref,
    gap_ref,
    ping_ref,
    pong_ref,
    spread_ref,
    keep_ref,
):
    top, end = HY, HY + RY
    zero = jnp.zeros((RY, LX), f32)
    cells = [tissue_rows(tissue_ref, 1, g) for g in range(GROUPS)]
    for g in range(GROUPS):
        own = cells[g]
        spread = smooth_rate * own
        spread_ref[g] = spread
        flat = 2.0 * own + pltpu.roll(own, 1, 0) + pltpu.roll(own, RY - 1, 0)
        below = cells[g - 1] if g else zero
        above = cells[g + 1] if g + 1 < GROUPS else zero
        keep_ref[3 * g] = 1.0 - spread * (flat + below + own)
        keep_ref[3 * g + 1] = 1.0 - spread * (flat + own + own)
        keep_ref[3 * g + 2] = 1.0 - spread * (flat + own + above)
    for ref in (ping_ref, pong_ref):
        for c in range(3):
            ref[c, 0, top:end] = zero
            ref[c, NZ + 1, top:end] = zero

    def put(ref, z, pulled):
        for c in range(3):
            ref[c, z + 1, top:end] = pulled[c]
            ref[c, z + 1, 0:top] = pulled[c][BY:]
            ref[c, z + 1, end : end + HY] = pulled[c][:HY]

    for z in range(NZ):
        m = moving_ref[z]
        above = moving_ref[z + 1] if z < NZ - 1 else zero
        below = moving_ref[z - 1] if z else zero
        s = [
            0.5 * (above - below),
            0.5 * (pltpu.roll(m, RY - 1, 0) - pltpu.roll(m, 1, 0)),
            0.5 * (pltpu.roll(m, LX - 1, 1) - pltpu.roll(m, 1, 1)),
        ]
        energy = energy_of(s)
        gap = ring(fixed_ref[z], after_ref[3, z], before_ref[3, z]) - m
        t = cells[z // ZG]
        field = [t * ring(field_ref[c, z], after_ref[c, z], before_ref[c, z]) for c in range(3)]
        put(ping_ref, z, attract(field, s, gap, energy, t))
        for c in range(3):
            slope_ref[c, z] = s[c]
        energy_ref[z] = energy
        gap_ref[z] = gap

    def smoothed(src, z, c, rows):
        def at(dz, dy):
            return src[c, z + 1 + dz, top + dy : top + dy + rows]

        p = at(0, 0)
        around = (
            (at(1, 0) + at(-1, 0)) + (at(0, 1) + at(0, -1)) + (pltpu.roll(p, 1, 1) + pltpu.roll(p, LX - 1, 1))
        )
        g, k = z // ZG, z % ZG
        keep = keep_ref[3 * g + (0 if k == 0 else 2 if k == ZG - 1 else 1), 0:rows]
        return keep * p + spread_ref[g, 0:rows] * around

    src, dst = ping_ref, pong_ref
    for sweep in range(ITERS - 1):
        for z in range(NZ):
            field = [smoothed(src, z, c, RY) for c in range(3)]
            s = [slope_ref[c, z] for c in range(3)]
            put(dst, z, attract(field, s, gap_ref[z], energy_ref[z], cells[z // ZG]))
        src, dst = dst, src
    for z in range(NZ):
        for c in range(3):
            out_ref[c, z] = smoothed(src, z, c, BY)


def core(tissue, moving, fixed, field, after, before):
    return pl.pallas_call(
        core_kernel,
        out_shape=jax.ShapeDtypeStruct((3, NZ, BY, LX), f32),
        in_specs=[smem] + [vmem] * 5,
        out_specs=vmem,
        scratch_shapes=[
            VMEM((3, NZ, RY, LX), f32),
            VMEM((NZ, RY, LX), f32),
            VMEM((NZ, RY, LX), f32),
            VMEM((3, NZ + 2, RY + 2 * HY, LX), f32),
            VMEM((3, NZ + 2, RY + 2 * HY, LX), f32),
            VMEM((GROUPS, RY, LX), f32),
            VMEM((3 * GROUPS, RY, LX), f32),
        ],
        compiler_params=params(16),
        cost_estimate=pl.CostEstimate(flops=10000000000, bytes_accessed=2**20, transcendentals=0),
        name="core",
    )(tissue, moving, fixed, field, after, before)


def chain_neighbours(chain):
    lane = iota((RY, LX), 1)
    j = lane % EX
    first, last = j == 0, j == EX - 1
    low, high = lane < EX, lane >= LX - EX
    above = [pltpu.roll(p, LX - EX, 1) for p in chain]
    below = [pltpu.roll(p, EX, 1) for p in chain]
    out = []
    for k, p in enumerate(chain):
        before = jnp.where(last, above[k - 1], p) if k else p
        after = jnp.where(first, below[k + 1], p) if k + 1 < len(chain) else p
        out.append(
            (
                jnp.where(high, 0.0, above[k]),
                jnp.where(low, 0.0, below[k]),
                pltpu.roll(p, RY - 1, 0),
                pltpu.roll(p, 1, 0),
                pltpu.roll(after, LX - 1, 1),
                pltpu.roll(before, 1, 1),
            )
        )
    return out


def total(neighbours):
    above, below, after_y, before_y, after_x, before_x = neighbours
    return ((above + below) + (after_y + before_y)) + (after_x + before_x)


def edge_kernel(
    tissue_ref,
    inside_ref,
    left_ref,
    left_in_ref,
    right_ref,
    right_in_ref,
    got_left_ref,
    got_right_ref,
    core_ref,
    out_ref,
):
    lane = iota((RY, LX), 1)

    def side(refs, columns, outer, inside):
        tissue = []
        for column in columns:
            cell = tissue_rows(tissue_ref, column, GROUPS - 1)
            for g in range(GROUPS - 2, -1, -1):
                cell = jnp.where(lane < (g + 1) * ZG * EX, tissue_rows(tissue_ref, column, g), cell)
            tissue.append(cell)
        spread = [smooth_rate * t for t in tissue]
        keep = [1.0 - b * total(n) for b, n in zip(spread, chain_neighbours(tissue))]
        moving = [ref[4] * inside if k == outer else ref[4] for k, ref in enumerate(refs)]
        slopes = [
            [0.5 * (n[0] - n[1]), 0.5 * (n[2] - n[3]), 0.5 * (n[4] - n[5])] for n in chain_neighbours(moving)
        ]
        energy = [energy_of(s) for s in slopes]
        gap = [ref[3] - m for ref, m in zip(refs, moving)]
        field = [[t * ref[c] for c in range(3)] for t, ref in zip(tissue, refs)]
        for sweep in range(ITERS):
            pulled = [attract(*x) for x in zip(field, slopes, gap, energy, tissue)]
            near = [chain_neighbours([p[c] for p in pulled]) for c in range(3)]
            field = [
                [keep[k] * pulled[k][c] + spread[k] * total(near[c][k]) for c in range(3)] for k in range(len(refs))
            ]
        return field[1]

    left = side((got_left_ref, left_ref, left_in_ref), (0, 1, 1), 0, inside_ref[0])
    right = side((right_in_ref, right_ref, got_right_ref), (1, 1, 2), 2, inside_ref[1])
    at_left, at_right = lane[:BY] < EX, lane[:BY] >= LX - EX
    for z in range(NZ):
        for c in range(3):
            a = pltpu.roll(left[c][:BY], (-EX * z) % LX, 1)
            b = pltpu.roll(right[c][:BY], (-EX * (z + 1)) % LX, 1)
            out_ref[c, z] = jnp.where(at_left, a, jnp.where(at_right, b, core_ref[c, z]))


def edge(tissue, inside, packs, got_left, got_right, middle):
    return pl.pallas_call(
        edge_kernel,
        out_shape=jax.ShapeDtypeStruct((3, NZ, BY, LX), f32),
        in_specs=[smem, smem] + [vmem] * 7,
        out_specs=vmem,
        compiler_params=params(16),
        name="edge",
    )(tissue, inside, *packs, got_left, got_right, middle)


def turn(x, axis, by):
    size = lax.axis_size(axis)
    return lax.ppermute(x, axis, [(i, (i + by) % size) for i in range(size)])


def body(moving_slab, fixed_image, start_field, tissue_mask):
    row = lax.axis_index("row")
    col = lax.axis_index("col")
    blocks = cut(moving_slab)
    moving = lax.all_to_all(blocks, "row", split_axis=0, concat_axis=0, tiled=True)

    state = jnp.concatenate([start_field, fixed_image[None]], axis=0)
    after = turn(state[:, :, 0 : HY // 2], "row", -1)
    before = turn(state[:, :, BY - HY // 2 :], "row", 1)

    padded = jnp.pad(tissue_mask, ((0, 0), (1, 1), (1, 1))).astype(f32)
    tissue = lax.dynamic_slice(padded, (0, row, col), (GROUPS, 3, 3)).reshape(-1)
    inside = jnp.stack([col > 0, col < lax.axis_size("col") - 1]).astype(f32)

    packs = pack(moving, fixed_image, start_field, after, before)
    left, _, right, _ = packs
    got_left = turn(right, "col", 1)
    got_right = turn(left, "col", -1)
    middle = core(tissue, moving, fixed_image, start_field, after, before)
    return edge(tissue, inside, packs, got_left, got_right, middle)


def solution(mesh):
    in_specs = (P("row", None, "col"), P(None, "row", "col"), P(None, None, "row", "col"), P())
    out_specs = P(None, None, "row", "col")
    return jax.shard_map(body, mesh=mesh, in_specs=in_specs, out_specs=out_specs, check_vma=False)
```

```python
import jax
import jax.numpy as jnp
from jax import lax
from jax.experimental import pallas as pl
from jax.experimental.pallas import tpu as pltpu
from jax.sharding import PartitionSpec as P

ITERS = 3
pull_rate = 1.0
smooth_rate = 0.16

NZ = 32
BY = 16
HY = 8
RY = BY + HY
LX = 128
EX = LX // NZ
ZG = 8
GROUPS = NZ // ZG

VMEM = pltpu.VMEM
f32 = jnp.float32
vmem = pl.BlockSpec(memory_space=VMEM)
smem = pl.BlockSpec(memory_space=pltpu.SMEM)


def params(mib):
    return pltpu.CompilerParams(vmem_limit_bytes=mib * 2**20)


def iota(shape, dim):
    return lax.broadcasted_iota(jnp.int32, shape, dim)


def cut_kernel(slab_ref, out_ref):
    count = slab_ref.shape[0]
    low = iota((HY, LX), 0) < HY // 2
    zero = jnp.zeros((HY, LX), f32)
    for i in range(count):
        after = slab_ref[i + 1, 0:HY] if i + 1 < count else zero
        before = slab_ref[i - 1, HY:BY] if i else zero
        out_ref[i, 0:BY] = slab_ref[i]
        out_ref[i, BY:RY] = jnp.where(low, after, before)


def cut(slab):
    count = slab.shape[1] // BY
    return pl.pallas_call(
        cut_kernel,
        out_shape=jax.ShapeDtypeStruct((count, RY, LX), f32),
        in_specs=[vmem],
        out_specs=vmem,
        compiler_params=params(4),
        name="cut",
    )(slab.reshape(count, BY, LX))


def chain_neighbours(chain):
    lane = iota((RY, LX), 1)
    j = lane % EX
    first, last = j == 0, j == EX - 1
    low, high = lane < EX, lane >= LX - EX
    above = [pltpu.roll(p, LX - EX, 1) for p in chain]
    below = [pltpu.roll(p, EX, 1) for p in chain]
    out = []
    for k, p in enumerate(chain):
        before = jnp.where(last, above[k - 1], p) if k else p
        after = jnp.where(first, below[k + 1], p) if k + 1 < len(chain) else p
        out.append(
            (
                jnp.where(high, 0.0, above[k]),
                jnp.where(low, 0.0, below[k]),
                pltpu.roll(p, RY - 1, 0),
                pltpu.roll(p, 1, 0),
                pltpu.roll(after, LX - 1, 1),
                pltpu.roll(before, 1, 1),
            )
        )
    return out


def total(neighbours):
    above, below, after_y, before_y, after_x, before_x = neighbours
    return ((above + below) + (after_y + before_y)) + (after_x + before_x)


def ring(core, after, before):
    return jnp.concatenate([core, after, before], axis=0)


def pack_rows(rows, refs, which):
    group = iota((RY, LX), 1) // EX
    packs = [jnp.zeros((RY, LX), f32)] * 4
    offsets = (1, 2, 0, -1)
    for z in range(NZ):
        turned = pltpu.roll(rows(z), (EX * (z + 1)) % LX, 1)
        packs = [jnp.where(group == (z + at) % NZ, turned, p) for at, p in zip(offsets, packs)]
    for at, p, ref in zip(offsets, packs, refs):
        ref[which] = pltpu.roll(p, (-EX * at) % LX, 1) if at else p


def tissue_rows(tissue_ref, column, group):
    row = iota((RY, LX), 0)

    def at(k):
        return tissue_ref[(group * 3 + k) * 3 + column]

    return jnp.where(row < BY, at(1), jnp.where(row < BY + HY // 2, at(2), at(0)))


def prepare_kernel(
    tissue_ref,
    inside_ref,
    fixed_ref,
    field_ref,
    after_ref,
    before_ref,
    left_ref,
    left_in_ref,
    right_ref,
    right_in_ref,
    cell_ref,
    keep_ref,
    edge_cell_ref,
    edge_keep_ref,
    edge_inside_ref,
):
    zero = jnp.zeros((RY, LX), f32)
    lane = iota((RY, LX), 1)
    cells = [tissue_rows(tissue_ref, 1, g) for g in range(GROUPS)]
    for g in range(GROUPS):
        own = cells[g]
        cell_ref[g] = own
        spread = smooth_rate * own
        flat = 2.0 * own + pltpu.roll(own, 1, 0) + pltpu.roll(own, RY - 1, 0)
        below = cells[g - 1] if g else zero
        above = cells[g + 1] if g + 1 < GROUPS else zero
        keep_ref[3 * g] = 1.0 - spread * (flat + below + own)
        keep_ref[3 * g + 1] = 1.0 - spread * (flat + own + own)
        keep_ref[3 * g + 2] = 1.0 - spread * (flat + own + above)
    for side, columns in enumerate(((0, 1, 1), (1, 1, 2))):
        edge_inside_ref[side] = jnp.full((RY, LX), inside_ref[side], f32)
        chain = []
        for column in columns:
            cell = tissue_rows(tissue_ref, column, GROUPS - 1)
            for g in range(GROUPS - 2, -1, -1):
                cell = jnp.where(lane < (g + 1) * ZG * EX, tissue_rows(tissue_ref, column, g), cell)
            chain.append(cell)
        for k, (t, near) in enumerate(zip(chain, chain_neighbours(chain))):
            edge_cell_ref[side, k] = t
            edge_keep_ref[side, k] = 1.0 - smooth_rate * t * total(near)
    for which in range(4):

        def rows(z):
            x = fixed_ref[z] if which == 3 else field_ref[which, z]
            x = ring(x, after_ref[which, z], before_ref[which, z])
            return x if which == 3 else cells[z // ZG] * x

        pack_rows(rows, (left_ref, left_in_ref, right_ref, right_in_ref), which)


def pack_moving_kernel(moving_ref, *refs):
    pack_rows(lambda z: moving_ref[z], refs[-4:], 4)


PACK = jax.ShapeDtypeStruct((5, RY, LX), f32)


def prepare(tissue, inside, fixed, field, after, before):
    def shape(*dims):
        return jax.ShapeDtypeStruct(dims + (RY, LX), f32)

    return pl.pallas_call(
        prepare_kernel,
        out_shape=(PACK,) * 4 + (shape(GROUPS), shape(3 * GROUPS), shape(2, 3), shape(2, 3), shape(2)),
        in_specs=[smem, smem] + [vmem] * 4,
        out_specs=(vmem,) * 9,
        compiler_params=params(8),
        cost_estimate=pl.CostEstimate(flops=20000000000, bytes_accessed=2**20, transcendentals=0),
        name="prepare",
    )(tissue, inside, fixed, field, after, before)


def pack_moving(moving, *packs):
    return pl.pallas_call(
        pack_moving_kernel,
        out_shape=(PACK,) * 4,
        in_specs=[vmem] * 5,
        out_specs=(vmem,) * 4,
        input_output_aliases={1: 0, 2: 1, 3: 2, 4: 3},
        compiler_params=params(4),
        name="pack_moving",
    )(moving, *packs)


def recip(x):
    r = pl.reciprocal(x, approx=True)
    return r * (2.0 - x * r)


def energy_of(s):
    return s[0] * s[0] + s[1] * s[1] + s[2] * s[2] + 0.5


def attract(field, slopes, gap, energy, tissue):
    residual = gap - (slopes[0] * field[0] + slopes[1] * field[1] + slopes[2] * field[2])
    rate = pull_rate * tissue * residual * recip(energy + residual * residual)
    return [field[c] + rate * slopes[c] for c in range(3)]


def core_kernel(
    moving_ref,
    fixed_ref,
    field_ref,
    after_ref,
    before_ref,
    cell_ref,
    keep_ref,
    out_ref,
    slope_ref,
    energy_ref,
    gap_ref,
    ping_ref,
    pong_ref,
):
    top, end = HY, HY + RY
    zero = jnp.zeros((RY, LX), f32)
    for ref in (ping_ref, pong_ref):
        for c in range(3):
            ref[c, 0, top:end] = zero
            ref[c, NZ + 1, top:end] = zero

    def put(ref, z, pulled):
        for c in range(3):
            ref[c, z + 1, top:end] = pulled[c]
            ref[c, z + 1, 0:top] = pulled[c][BY:]
            ref[c, z + 1, end : end + HY] = pulled[c][:HY]

    for z in range(NZ):
        m = moving_ref[z]
        above = moving_ref[z + 1] if z < NZ - 1 else zero
        below = moving_ref[z - 1] if z else zero
        s = [
            0.5 * (above - below),
            0.5 * (pltpu.roll(m, RY - 1, 0) - pltpu.roll(m, 1, 0)),
            0.5 * (pltpu.roll(m, LX - 1, 1) - pltpu.roll(m, 1, 1)),
        ]
        energy = energy_of(s)
        gap = ring(fixed_ref[z], after_ref[3, z], before_ref[3, z]) - m
        t = cell_ref[z // ZG]
        field = [t * ring(field_ref[c, z], after_ref[c, z], before_ref[c, z]) for c in range(3)]
        put(ping_ref, z, attract(field, s, gap, energy, t))
        for c in range(3):
            slope_ref[c, z] = s[c]
        energy_ref[z] = energy
        gap_ref[z] = gap

    def smoothed(src, z, c, rows):
        def at(dz, dy):
            return src[c, z + 1 + dz, top + dy : top + dy + rows]

        p = at(0, 0)
        around = (
            (at(1, 0) + at(-1, 0)) + (at(0, 1) + at(0, -1)) + (pltpu.roll(p, 1, 1) + pltpu.roll(p, LX - 1, 1))
        )
        g, k = z // ZG, z % ZG
        keep = keep_ref[3 * g + (0 if k == 0 else 2 if k == ZG - 1 else 1), 0:rows]
        return keep * p + (smooth_rate * cell_ref[g, 0:rows]) * around

    src, dst = ping_ref, pong_ref
    for sweep in range(ITERS - 1):
        for z in range(NZ):
            field = [smoothed(src, z, c, RY) for c in range(3)]
            s = [slope_ref[c, z] for c in range(3)]
            put(dst, z, attract(field, s, gap_ref[z], energy_ref[z], cell_ref[z // ZG]))
        src, dst = dst, src
    for z in range(NZ):
        for c in range(3):
            out_ref[c, z] = smoothed(src, z, c, BY)


def core(moving, fixed, field, after, before, cell, keep):
    return pl.pallas_call(
        core_kernel,
        out_shape=jax.ShapeDtypeStruct((3, NZ, BY, LX), f32),
        in_specs=[vmem] * 7,
        out_specs=vmem,
        scratch_shapes=[
            VMEM((3, NZ, RY, LX), f32),
            VMEM((NZ, RY, LX), f32),
            VMEM((NZ, RY, LX), f32),
            VMEM((3, NZ + 2, RY + 2 * HY, LX), f32),
            VMEM((3, NZ + 2, RY + 2 * HY, LX), f32),
        ],
        compiler_params=params(16),
        cost_estimate=pl.CostEstimate(flops=10000000000, bytes_accessed=2**20, transcendentals=0),
        name="core",
    )(moving, fixed, field, after, before, cell, keep)


def edge_kernel(
    left_ref,
    left_in_ref,
    right_ref,
    right_in_ref,
    got_left_ref,
    got_right_ref,
    cell_ref,
    keep_ref,
    inside_ref,
    core_ref,
    out_ref,
):
    lane = iota((RY, LX), 1)
    chains = ((got_left_ref, left_ref, left_in_ref), (right_in_ref, right_ref, got_right_ref))
    moving = [
        [chains[0][0][4] * inside_ref[0], chains[0][1][4], chains[0][2][4]],
        [chains[1][0][4], chains[1][1][4], chains[1][2][4] * inside_ref[1]],
    ]
    tissue = [[cell_ref[e, k] for k in range(3)] for e in range(2)]
    slopes = [
        [[0.5 * (n[0] - n[1]), 0.5 * (n[2] - n[3]), 0.5 * (n[4] - n[5])] for n in chain_neighbours(m)] for m in moving
    ]
    energy = [[energy_of(x) for x in s] for s in slopes]
    gap = [[ref[3] - x for ref, x in zip(refs, m)] for refs, m in zip(chains, moving)]
    field = [[[t * ref[c] for c in range(3)] for t, ref in zip(ts, refs)] for ts, refs in zip(tissue, chains)]
    for sweep in range(ITERS):
        pulled = [
            [attract(*x) for x in zip(field[e], slopes[e], gap[e], energy[e], tissue[e])] for e in range(2)
        ]
        near = [[chain_neighbours([p[c] for p in pulled[e]]) for c in range(3)] for e in range(2)]
        field = [
            [
                [keep_ref[e, k] * pulled[e][k][c] + smooth_rate * tissue[e][k] * total(near[e][c][k]) for c in range(3)]
                for k in range(3)
            ]
            for e in range(2)
        ]
    left, right = field[0][1], field[1][1]
    even = (lane // EX)[:BY] % 2 == 0
    outer = (lane[:BY] < EX) | (lane[:BY] >= LX - EX)
    both = [[], []]
    for c in range(3):
        a, b = left[c][:BY], right[c][:BY]
        both[0].append(jnp.where(even, b, pltpu.roll(a, EX, 1)))
        both[1].append(jnp.where(even, pltpu.roll(b, LX - EX, 1), a))
    for z in range(NZ):
        for c in range(3):
            turned = pltpu.roll(both[z % 2][c], (-EX * (z // 2 * 2 + 1)) % LX, 1)
            out_ref[c, z] = jnp.where(outer, turned, core_ref[c, z])


def edge(packs, got_left, got_right, weights, middle):
    return pl.pallas_call(
        edge_kernel,
        out_shape=jax.ShapeDtypeStruct((3, NZ, BY, LX), f32),
        in_specs=[vmem] * 10,
        out_specs=vmem,
        compiler_params=params(16),
        name="edge",
    )(*packs, got_left, got_right, *weights, middle)


def turn(x, axis, by):
    size = lax.axis_size(axis)
    return lax.ppermute(x, axis, [(i, (i + by) % size) for i in range(size)])


def body(moving_slab, fixed_image, start_field, tissue_mask):
    row = lax.axis_index("row")
    col = lax.axis_index("col")
    blocks = cut(moving_slab)
    moving = lax.all_to_all(blocks, "row", split_axis=0, concat_axis=0, tiled=True)

    state = jnp.concatenate([start_field, fixed_image[None]], axis=0)
    after = turn(state[:, :, 0 : HY // 2], "row", -1)
    before = turn(state[:, :, BY - HY // 2 :], "row", 1)

    padded = jnp.pad(tissue_mask, ((0, 0), (1, 1), (1, 1))).astype(f32)
    tissue = lax.dynamic_slice(padded, (0, row, col), (GROUPS, 3, 3)).reshape(-1)
    inside = jnp.stack([col > 0, col < lax.axis_size("col") - 1]).astype(f32)

    prepared = prepare(tissue, inside, fixed_image, start_field, after, before)
    cell, keep, *weights = prepared[4:]
    packs = pack_moving(moving, *prepared[:4])
    left, _, right, _ = packs
    got_left = turn(right, "col", 1)
    got_right = turn(left, "col", -1)
    middle = core(moving, fixed_image, start_field, after, before, cell, keep)
    return edge(packs, got_left, got_right, weights, middle)


def solution(mesh):
    in_specs = (P("row", None, "col"), P(None, "row", "col"), P(None, None, "row", "col"), P())
    out_specs = P(None, None, "row", "col")
    return jax.shard_map(body, mesh=mesh, in_specs=in_specs, out_specs=out_specs, check_vma=False)
```
